256 devices in a mesh: expert: 32 (over x, z), mp: 8 (over y, core).
Axes of the slice: x: 4, y: 4, z: 8, core: 2. Of those that a mesh axis runs over, the one named last changes fastest.
Arguments:
- activations: bfloat16 [4096, 8192], P('expert'), may hold values from -6 to 6
- out_grad: bfloat16 [4096, 8192], P('expert'), may hold values from -1.5 to 1.5
- expert_ids: int32 [4096, 2], P('expert'), may hold values from 0 to 31, all different within a row; in each aligned block of 128 rows (0 to 127, 128 to 255, ...) at most 16 rows name the same one
- gate_probs: float32 [4096, 2], P('expert'), may hold values from 0.1 to 1
- keep_mask: int32 [4096, 2], P('expert'), may hold values 0 or 1
- w_input: bfloat16 [32, 8192, 1024], P('expert', None, 'mp'), may hold values from -0.1875 to 0.1875
- w_output: bfloat16 [32, 1024, 8192], P('expert', 'mp'), may hold values from -0.0625 to 0.0625
Outputs:
- grad_tokens: bfloat16 [4096, 8192], P('expert', 'mp')
- grad_win: bfloat16 [32, 8192, 1024], P('expert', None, 'mp')
- grad_wout: bfloat16 [32, 1024, 8192], P('expert', 'mp')
The draws below stay inside these ranges and needn't reach their ends.
Inputs may be any that keep to these rules, and one draw needn't show every extreme that they name: `expert_ids`: each token names two different experts. Within each aligned block of 128 tokens no expert is named by more than 16 tokens, a bound that some block reaches.
All inputs are finite; a program needn't handle non-finite values. No bound on the sum of `keep_mask` on one device may be relied on, other than what follows from the above.
Results may differ from the reference program's by a relative error of at most 0.019.
Values may be sent and summed in bfloat16 or wider, within the bound.
A program may use at most 128 MiB of HBM per device.

```python
import math
import jax
import jax.numpy as jnp
import numpy as np
from jax import lax

D = 8192
FF_DEV = 128
TOK_DEV = 128
EXPERTS = 32
FF = 1024
TOKENS = 4096
CAP = 16
N_EXPERT = 32
N_MP = 8


def plant(values, stream_key, least, top_value):
    shape = values.shape
    index_at = [jax.random.randint(jax.random.fold_in(stream_key, axis), (), 0, shape[axis]) for axis in range(len(shape))]
    values = values.at[tuple(index_at)].set(least)
    longest = shape.index(max(shape))
    index_at[longest] = (index_at[longest] + 1) % shape[longest]
    return values.at[tuple(index_at)].set(top_value)


def block_levels(own_key, dims, pieces, smallest, top_value):
    loudness = 1.0
    for axis_at, blocks in pieces:
        steps = jax.random.uniform(jax.random.fold_in(jax.random.fold_in(own_key, 6), axis_at), (blocks,), jnp.float32, smallest / len(pieces), top_value / len(pieces))
        loudness = loudness * jnp.repeat(jnp.exp(steps), dims[axis_at] // blocks).reshape((-1,) + (1,) * (len(dims) - 1 - axis_at))
    return loudness


def shared_out(own_key, own, number, rows, count, top, most, lean):
    sequence = jax.random.permutation(own_key, count)
    packed, common = portions_of(count, rows * top, most, lean, True), portions_of(count, rows * top, most, lean, False)
    places = jnp.arange(count)

    def named(sizes, rotation):
        used = int((sizes > 0).sum())
        fixed = max(1, used // 4)
        moved = fixed + (places - fixed + rotation * (used - fixed)) % max(1, count - fixed)
        return jnp.zeros((count,), jnp.int32).at[sequence[jnp.where(places < fixed, places, moved)]].set(jnp.asarray(sizes, jnp.int32))

    sizes = jnp.where(number % 4 == 0, named(packed, number // 4), named(common, number - number // 4 - 1))
    mixed = jax.random.permutation(jax.random.fold_in(own, 3), count)
    giver, taker = mixed[0:count // 2 * 2:2], mixed[1:count // 2 * 2:2]
    margin = jnp.minimum(sizes[giver] - 1, most - sizes[taker]) // 2
    margin = jnp.where((giver == sequence[0]) | (taker == sequence[0]) | (sizes[taker] == 0), 0, jnp.maximum(margin, 0))
    moved = jax.random.randint(jax.random.fold_in(own, 4), (count // 2,), 0, 1 << 20) % (margin + 1)
    sizes = sizes.at[giver].add(-moved).at[taker].add(moved)
    labels = jnp.searchsorted(jnp.cumsum(sizes), jnp.arange(rows * top), side="right").astype(jnp.int32)
    table = labels.reshape(top, rows).T
    table = table[jax.random.permutation(jax.random.fold_in(own, 1), rows)]
    rotation = jax.random.randint(jax.random.fold_in(own, 2), (rows, 1), 0, top)
    return jnp.take_along_axis(table, (jnp.arange(top)[None, :] + rotation) % top, axis=1)


def portions_of(count, total, reach, lean, full):
    portions = [(1 << 20) // math.isqrt(standing ** lean) + 1 for standing in range(1, count + 1)]
    largest = reach if full else min(reach, max(-(-total // count), total * portions[0] // sum(portions)))
    least = 1 if total - largest >= count - 1 else 0
    given, rest = [largest] + [least] * (count - 1), total - largest - least * (count - 1)
    while rest > 0:
        free = [i for i in range(1, count) if given[i] < largest] or [i for i in range(1, count) if given[i] < reach]
        whole, budget = sum([portions[i] for i in free]), rest
        for i in free:
            more = min(reach - given[i], max(1, budget * portions[i] // whole), rest)
            given[i] = given[i] + more
            rest = rest - more
    return np.array(given)


def centred(rng, shape, deviation, most, shards=(), kind=jnp.bfloat16):
    factor_of = block_levels(rng, shape, shards, -0.22, 0.18) if shards else 1.0
    values = jax.random.normal(rng, shape, jnp.float32) * deviation * factor_of
    return jnp.minimum(jnp.maximum(values, -most), most).astype(kind)


def setup_inputs(seed: int = 0) -> dict:
    seeds = jax.random.split(jax.random.key(seed), 8)
    activations = centred(seeds[0], (TOKENS, D), 1.0, 6.0, ((0, 32),))
    out_grad = centred(seeds[1], (TOKENS, D), 0.25, 1.5, ((0, 32),))
    expert_ids_keys = jax.random.split(jax.random.fold_in(seeds[2], 1), TOKENS // TOK_DEV)
    expert_ids_turns = jax.random.permutation(jax.random.fold_in(seeds[2], 3), TOKENS // TOK_DEV)
    expert_ids = jax.vmap(lambda own, number: shared_out(jax.random.fold_in(seeds[2], 2), own, number, TOK_DEV, EXPERTS, 2, CAP, 2))(expert_ids_keys, expert_ids_turns).reshape((TOKENS, 2))
    gate_probs = jnp.clip(0.1 + 0.9 * jax.random.uniform(seeds[3], (TOKENS, 2), jnp.float32) ** block_levels(seeds[3], (TOKENS, 2), ((0, 32),), -0.2, 0.2), 0.1, 1.0)
    keep_mask = plant((jax.random.randint(seeds[4], (TOKENS, 2), 0, 8) < 7).astype(jnp.int32), jax.random.fold_in(seeds[4], 1), 0, 1)
    w_input = centred(seeds[5], (EXPERTS, D, FF), FF ** -0.5, 0.1875, ((0, 32), (2, 8)))
    w_output = centred(seeds[6], (EXPERTS, FF, D), D ** -0.5, 0.0625, ((0, 32), (1, 8)))
    return {"activations": activations, "out_grad": out_grad, "expert_ids": expert_ids, "gate_probs": gate_probs, "keep_mask": keep_mask, "w_input": w_input, "w_output": w_output}


def contract_rows(left, right):
    return lax.dot_general(left, right, (((0,), (0,)), ((), ())), preferred_element_type=jnp.float32)

def contract_cols(left, right):
    return lax.dot_general(left, right, (((1,), (1,)), ((), ())), preferred_element_type=jnp.float32)

def reference(activations, out_grad, expert_ids, gate_probs, keep_mask, w_input, w_output):
    rows_total = N_EXPERT * CAP
    grouped = expert_ids.reshape(N_EXPERT, TOK_DEV * 2)
    chosen = (grouped[:, :, None] == jnp.arange(EXPERTS, dtype=jnp.int32)[None, None, :]).astype(jnp.int32)
    slots = lax.optimization_barrier(jnp.sum(chosen * (jnp.cumsum(chosen, axis=1) - 1), axis=2)).reshape(TOKENS, 2)
    blocks = (jnp.arange(TOKENS, dtype=jnp.int32) // TOK_DEV)[:, None]
    rows_of = (blocks * CAP + slots).astype(jnp.int32)
    entries = (jnp.arange(TOKENS * 2, dtype=jnp.int32) + 1).reshape(TOKENS, 2)
    weights_k = gate_probs * keep_mask.astype(jnp.float32)

    def step(carry, inputs):
        expert, weight_in, weight_out = inputs
        target = jnp.where(expert_ids == expert, rows_of, rows_total).astype(jnp.int32)
        owner = jax.ops.segment_sum(entries.reshape(-1), target.reshape(-1), num_segments=rows_total + 1)[:rows_total]
        filled = owner > 0
        index = jnp.maximum(owner - 1, 0).astype(jnp.int32)
        token = index // 2
        member = index % 2
        rows_x = jnp.where(filled[:, None], activations[token], jnp.zeros((), jnp.bfloat16)).astype(jnp.bfloat16)
        factor = jnp.where(filled, weights_k[token, member], jnp.float32(0.0))
        rows_g = (factor[:, None] * out_grad[token].astype(jnp.float32)).astype(jnp.bfloat16)
        hidden = jnp.dot(rows_x, weight_in, preferred_element_type=jnp.float32)
        active, pullback = jax.vjp(jax.nn.gelu, hidden)
        active = active.astype(jnp.bfloat16)
        grad_wout = contract_rows(active, rows_g).astype(jnp.bfloat16)
        grad_act = contract_cols(rows_g, weight_out)
        grad_hidden = pullback(grad_act)[0].astype(jnp.bfloat16)
        grad_win = contract_rows(rows_x, grad_hidden).astype(jnp.bfloat16)
        grad_rows = jnp.zeros((rows_total, D), jnp.float32)
        for block in range(N_MP):
            part = contract_cols(grad_hidden[:, block * FF_DEV:(block + 1) * FF_DEV], weight_in[:, block * FF_DEV:(block + 1) * FF_DEV])
            part = lax.optimization_barrier(part.astype(jnp.bfloat16))
            grad_rows = grad_rows + part.astype(jnp.float32)
        carry = carry.at[token].add(jnp.where(filled[:, None], grad_rows, jnp.float32(0.0)))
        return (carry, (grad_win, grad_wout))
    start = jnp.zeros((TOKENS, D), jnp.float32)
    total, (grad_win, grad_wout) = lax.scan(step, start, (jnp.arange(EXPERTS, dtype=jnp.int32), w_input, w_output))
    return (total.astype(jnp.bfloat16), grad_win, grad_wout)
```

```python
import jax
import jax.numpy as jnp
from jax import lax
from jax.sharding import PartitionSpec as P


def contract_rows(left, right):
    return lax.dot_general(
        left, right, (((0,), (0,)), ((), ())), preferred_element_type=jnp.float32
    )


def contract_cols(left, right):
    return lax.dot_general(
        left, right, (((1,), (1,)), ((), ())), preferred_element_type=jnp.float32
    )


def slot_rows(expert_ids, experts, capacity):
    flat = expert_ids.reshape(-1)
    chosen = (flat[:, None] == jnp.arange(experts, dtype=jnp.int32)[None, :]).astype(jnp.int32)
    earlier = jnp.cumsum(chosen, axis=0) - 1
    slots = jnp.sum(chosen * earlier, axis=1).reshape(expert_ids.shape)
    return expert_ids * capacity + slots


def local(activations, out_grad, expert_ids, gate_probs, keep_mask, w_input, w_output):
    experts = lax.axis_size("expert")
    parts = lax.axis_size("mp")
    me = lax.axis_index("mp")
    tok_rows, model_dim = activations.shape
    width = model_dim // parts
    capacity = 4 * tok_rows // experts
    rows_total = experts * capacity
    places = slot_rows(expert_ids, experts, capacity)
    lanes = jnp.arange(rows_total, dtype=jnp.int32)[:, None]
    hit = [places[:, k][None, :] == lanes for k in range(2)]
    select = (hit[0] | hit[1]).astype(jnp.bfloat16)
    weights_k = gate_probs * keep_mask.astype(jnp.float32)
    factor = sum(
        jnp.sum(jnp.where(hit[k], weights_k[:, k][None, :], 0.0), axis=1, keepdims=True)
        for k in range(2)
    )
    mine_x = lax.dynamic_slice(activations, (0, me * width), (tok_rows, width))
    mine_g = lax.dynamic_slice(out_grad, (0, me * width), (tok_rows, width))
    sent_x = jnp.dot(select, mine_x, preferred_element_type=jnp.float32).astype(jnp.bfloat16)
    sent_g = (factor * jnp.dot(select, mine_g, preferred_element_type=jnp.float32)).astype(jnp.bfloat16)
    sent = jnp.stack([sent_x, sent_g], axis=1).reshape(experts, capacity * 2 * width // 128, 128)
    recv = lax.all_to_all(sent, "expert", split_axis=0, concat_axis=0, tiled=True)
    recv = recv.reshape(rows_total, 2, width)
    rows_x = lax.all_gather(recv[:, 0], "mp", axis=1, tiled=True)
    rows_g = lax.all_gather(recv[:, 1], "mp", axis=1, tiled=True)
    weight_in = w_input[0]
    weight_out = w_output[0]
    hidden = jnp.dot(rows_x, weight_in, preferred_element_type=jnp.float32)
    active, pullback = jax.vjp(jax.nn.gelu, hidden)
    active = active.astype(jnp.bfloat16)
    grad_wout = contract_rows(active, rows_g).astype(jnp.bfloat16)
    grad_act = contract_cols(rows_g, weight_out)
    grad_hidden = pullback(grad_act)[0].astype(jnp.bfloat16)
    grad_win = contract_rows(rows_x, grad_hidden).astype(jnp.bfloat16)
    grad_rows = contract_cols(grad_hidden, weight_in).astype(jnp.bfloat16)
    summed = lax.psum_scatter(grad_rows, "mp", scatter_dimension=1, tiled=True)
    returned = lax.all_to_all(
        summed.reshape(experts, capacity, width), "expert", split_axis=0, concat_axis=0, tiled=True
    ).reshape(rows_total, width)
    grad_tokens = contract_rows(select, returned).astype(jnp.bfloat16)
    return (grad_tokens, grad_win[None], grad_wout[None])


def solution(mesh):
    return jax.shard_map(
        local,
        mesh=mesh,
        in_specs=(
            P("expert", None),
            P("expert", None),
            P("expert", None),
            P("expert", None),
            P("expert", None),
            P("expert", None, "mp"),
            P("expert", "mp", None),
        ),
        out_specs=(P("expert", "mp"), P("expert", None, "mp"), P("expert", "mp", None)),
        check_vma=False,
    )
```

```python
import functools
import math
import jax
import jax.numpy as jnp
from jax import lax
from jax.sharding import PartitionSpec as P
import jax.experimental.pallas as pl
import jax.experimental.pallas.tpu as pltpu

CAP = 16
NY = 4
GRID = {32: (4, 8)}
MESH = pl.DeviceIdType.MESH
SCALE = math.sqrt(2.0 / math.pi)
CUBE = 0.044715


def contract_cols(left, right):
    return lax.dot_general(
        left, right, (((1,), (1,)), ((), ())), preferred_element_type=jnp.float32
    )


def product(left, right):
    return jnp.dot(left, right, preferred_element_type=jnp.float32)


def wrap(value, size):
    return lax.rem(value + size, size)


def kernel(
    nx, nz,
    ids_ref, weight_ref, act_hbm, grad_hbm, win_hbm, wout_hbm,
    tokens_out, gwin_hbm, gwout_hbm,
    act_v, grad_v, sent, rows, win_v, wout_v, win_all, hid_grad, active_v,
    back_sent, back, gwin_v, gwout_v,
    load_sem, win_send, win_recv, out_send, out_recv, ring_send, left_recv, right_recv,
    far_recv, core_recv, hid_send, hid_recv, back_send, back_recv, store_sem,
):
    experts = nx * nz
    toks, width = act_v.shape
    parts = rows.shape[0]
    total = sent.shape[0]
    span = nz * CAP
    half = span // 2
    ff = win_v.shape[1]
    me_e = lax.axis_index("expert")
    me_m = lax.axis_index("mp")
    mx, mz = me_e // nz, lax.rem(me_e, nz)
    my, mc = me_m // 2, lax.rem(me_m, 2)

    def expert_at(dx, dz):
        return {"expert": lax.rem(mx + dx, nx) * nz + lax.rem(mz + dz, nz)}

    def mate_at(dy, dc):
        return lax.rem(my + dy, NY) * 2 + lax.rem(mc + dc, 2)

    right, left, far = mate_at(1, 0), mate_at(NY - 1, 0), mate_at(2, 0)
    other = mate_at(0, 1)

    col = pl.multiple_of(me_m * width, width)
    loads = [
        pltpu.make_async_copy(act_hbm.at[:, pl.ds(col, width)], act_v, load_sem.at[0]),
        pltpu.make_async_copy(grad_hbm.at[:, pl.ds(col, width)], grad_v, load_sem.at[1]),
        pltpu.make_async_copy(win_hbm, win_v, load_sem.at[2]),
        pltpu.make_async_copy(wout_hbm, wout_v, load_sem.at[3]),
    ]
    for load in loads:
        load.start()

    barrier = pltpu.get_barrier_semaphore()

    @pl.loop(1, experts)
    def _(step):
        pl.semaphore_signal(
            barrier, inc=1, device_id=expert_at(step // nz, lax.rem(step, nz)), device_id_type=MESH
        )

    @pl.loop(1, parts)
    def _(step):
        pl.semaphore_signal(
            barrier, inc=1, device_id={"mp": lax.rem(me_m + step, parts)}, device_id_type=MESH
        )

    ids = ids_ref[...]
    weights = weight_ref[...]
    lane_e = lax.broadcasted_iota(jnp.int32, (experts, toks), 0)
    chosen = [(lane_e == ids[k : k + 1, :]).astype(jnp.float32) for k in range(2)]
    before = lax.broadcasted_iota(jnp.int32, (toks, toks), 0)
    after = lax.broadcasted_iota(jnp.int32, (toks, toks), 1)
    upper = (before < after).astype(jnp.bfloat16)
    earlier = product((chosen[0] + chosen[1]).astype(jnp.bfloat16), upper)
    dx = (ids >> int(math.log2(nz))) - mx
    dx = jnp.where(dx < 0, dx + nx, dx)
    dz = (ids & (nz - 1)) - mz
    dz = jnp.where(dz < 0, dz + nz, dz)
    base = (dx * nz + dz) * CAP
    places = [
        base[k : k + 1, :]
        + jnp.sum(chosen[k] * earlier, axis=0, keepdims=True).astype(jnp.int32)
        for k in range(2)
    ]

    def select(start, count):
        lanes = lax.broadcasted_iota(jnp.int32, (count, toks), 0) + start
        hit = [lanes == places[k] for k in range(2)]
        picked = jnp.logical_or(hit[0], hit[1])
        factor = jnp.where(hit[0], weights[0:1, :], 0.0) + jnp.where(hit[1], weights[1:2, :], 0.0)
        return picked, jnp.sum(factor, axis=1, keepdims=True)

    pl.semaphore_wait(barrier, experts - 1 + parts - 1)

    keep_win = pltpu.make_async_copy(
        win_hbm.at[pl.ds(col, width)], win_all.at[me_m], win_recv
    )
    keep_win.start()

    @pl.loop(1, parts)
    def _(step):
        mate = lax.rem(me_m + step, parts)
        start = pl.multiple_of(mate * width, width)
        pltpu.make_async_remote_copy(
            win_hbm.at[pl.ds(start, width)], win_all.at[me_m], win_send, win_recv,
            device_id={"mp": mate}, device_id_type=MESH,
        ).start()

    loads[0].wait()
    loads[1].wait()
    for k in range(nx):
        first = k * span
        picked, factor = select(first, span)
        picked = picked.astype(jnp.float32).astype(jnp.bfloat16)
        sent[pl.ds(first, span), pl.ds(0, width)] = product(picked, act_v[...]).astype(jnp.bfloat16)
        sent[pl.ds(first, span), pl.ds(width, width)] = (
            factor * product(picked, grad_v[...])
        ).astype(jnp.bfloat16)
        if k == 0:
            pltpu.make_async_copy(
                sent.at[pl.ds(0, CAP)], rows.at[me_m, pl.ds(0, CAP)], out_recv.at[0]
            ).start()

        @pl.loop(1 if k == 0 else 0, nz)
        def _(step):
            at = pl.ds(pl.multiple_of(first + step * CAP, CAP), CAP)
            pltpu.make_async_remote_copy(
                sent.at[at], rows.at[me_m, at], out_send.at[k], out_recv.at[k],
                device_id=expert_at(k, step), device_id_type=MESH,
            ).start()

    ring = []

    def pass_on(kind, k, slot, start, count, recv, mate):
        copy = pltpu.make_async_remote_copy(
            rows.at[slot, pl.ds(start, count)], rows.at[slot, pl.ds(start, count)],
            ring_send.at[kind, k], recv, device_id={"mp": mate}, device_id_type=MESH,
        )
        copy.start()
        ring.append(copy)

    def arrived(ref, sem):
        pltpu.make_async_copy(ref, ref, sem).wait()

    def stage_own(k):
        at = k * span
        arrived(rows.at[me_m, pl.ds(at, span)], out_recv.at[k])
        pass_on(0, k, me_m, at, span, left_recv.at[k], right)
        pass_on(1, k, me_m, at, span, right_recv.at[k], left)
        pass_on(2, k, me_m, at, span, core_recv.at[k], other)

    def stage_near(k):
        at = k * span
        arrived(rows.at[left, pl.ds(at, span)], left_recv.at[k])
        pass_on(3, k, left, at, half, far_recv.at[0, k], right)
        pass_on(4, k, left, at, span, core_recv.at[k], other)
        arrived(rows.at[right, pl.ds(at, span)], right_recv.at[k])
        pass_on(5, k, right, at + half, half, far_recv.at[1, k], left)
        pass_on(6, k, right, at, span, core_recv.at[k], other)

    def stage_far(k):
        at = k * span
        arrived(rows.at[far, pl.ds(at, half)], far_recv.at[0, k])
        arrived(rows.at[far, pl.ds(at + half, half)], far_recv.at[1, k])
        pass_on(7, k, far, at, span, core_recv.at[k], other)

    def stage_hidden(k):
        at = k * span
        arrived(rows.at[pl.ds(0, NY), pl.ds(at, span)], core_recv.at[k])
        if k == 0:
            loads[2].wait()
            loads[3].wait()

        def add(part, sums):
            hidden, grad_act = sums
            here = pl.ds(pl.multiple_of(part * width, width), width)
            block = rows[part, pl.ds(at, span), :]
            hidden = hidden + product(block[:, :width], win_v[here, :])
            grad_act = grad_act + contract_cols(block[:, width:], wout_v[:, here])
            return hidden, grad_act

        zero = jnp.zeros((span, ff), jnp.float32)
        hidden, grad_act = lax.fori_loop(0, parts, add, (zero, zero))
        square = hidden * hidden
        tanh = jnp.tanh(SCALE * (hidden + CUBE * (square * hidden)))
        active = 0.5 * hidden * (1.0 + tanh)
        slope = 0.5 * (1.0 + tanh) + 0.5 * hidden * (1.0 - tanh * tanh) * (
            SCALE * (1.0 + 3.0 * CUBE * square)
        )
        active_v[pl.ds(at, span), :] = active.astype(jnp.bfloat16)
        hid_grad[me_m, pl.ds(at, span), :] = (grad_act * slope).astype(jnp.bfloat16)

        @pl.loop(1, parts)
        def _(step):
            pltpu.make_async_remote_copy(
                hid_grad.at[me_m, pl.ds(at, span)], hid_grad.at[me_m, pl.ds(at, span)],
                hid_send.at[k], hid_recv.at[k],
                device_id={"mp": lax.rem(me_m + step, parts)}, device_id_type=MESH,
            ).start()

    def stage_back(k):
        at = k * span
        if k == 0:
            arrived(win_all, win_recv)
        arrived(hid_grad.at[pl.ds(0, parts - 1), pl.ds(at, span)], hid_recv.at[k])
        grads = jnp.concatenate([hid_grad[s, pl.ds(at, span), :] for s in range(parts)], axis=1)
        tile = min(256, width)

        @pl.loop(0, width // tile)
        def _(step):
            here = pl.ds(pl.multiple_of(step * tile, tile), tile)
            block = jnp.concatenate([win_all[s, here, :] for s in range(parts)], axis=1)
            back_sent[pl.ds(at, span), here] = contract_cols(grads, block).astype(jnp.bfloat16)

        if k == 0:
            pltpu.make_async_copy(
                back_sent.at[pl.ds(0, CAP)], back.at[pl.ds(0, CAP)], back_recv
            ).start()

        @pl.loop(1 if k == 0 else 0, nz)
        def _(step):
            here = pl.ds(pl.multiple_of(at + step * CAP, CAP), CAP)
            pltpu.make_async_remote_copy(
                back_sent.at[here], back.at[here], back_send, back_recv,
                device_id=expert_at(nx - k, nz - step), device_id_type=MESH,
            ).start()

    for step in range(nx + 4):
        if step < nx:
            stage_own(step)
        if 0 <= step - 1 < nx:
            stage_near(step - 1)
        if 0 <= step - 2 < nx:
            stage_far(step - 2)
        if 0 <= step - 3 < nx:
            stage_hidden(step - 3)
        if 0 <= step - 4 < nx:
            stage_back(step - 4)

    active_t = active_v[...].astype(jnp.float32).T.astype(jnp.bfloat16)
    hid_t = hid_grad[me_m].astype(jnp.float32).T.astype(jnp.bfloat16)
    tile = min(512, width)

    @pl.loop(0, parts)
    def _(part):
        for piece in range(width // tile):
            here = pl.ds(pl.multiple_of(part * width + piece * tile, tile), tile)
            gwout_v[:, here] = product(
                active_t, rows[part, :, pl.ds(width + piece * tile, tile)]
            ).astype(jnp.bfloat16)
            gwin_v[here, :] = product(
                hid_t, rows[part, :, pl.ds(piece * tile, tile)]
            ).T.astype(jnp.bfloat16)

    stores = [
        pltpu.make_async_copy(gwin_v, gwin_hbm, store_sem.at[0]),
        pltpu.make_async_copy(gwout_v, gwout_hbm, store_sem.at[1]),
    ]
    for store in stores:
        store.start()

    arrived(back, back_recv)
    for k in range(nx):
        picked, _ = select(k * span, span)
        picked_t = picked.astype(jnp.float32).T.astype(jnp.bfloat16)
        term = product(picked_t, back[pl.ds(k * span, span), :])
        sums = term if k == 0 else sums + term
    tokens_out[...] = sums.astype(jnp.bfloat16)

    for k in range(nx):
        lo = CAP if k == 0 else k * span
        gone = sent.at[pl.ds(lo, (k + 1) * span - lo)]
        arrived(gone, out_send.at[k])
        sent_hid = hid_grad.at[pl.ds(0, parts - 1), pl.ds(k * span, span)]
        arrived(sent_hid, hid_send.at[k])
    for copy in ring:
        copy.wait_send()
    arrived(win_all.at[pl.ds(0, parts - 1)], win_send)
    gone = back_sent.at[pl.ds(CAP, total - CAP)]
    arrived(gone, back_send)
    for store in stores:
        store.wait()


def local(grid, activations, out_grad, expert_ids, gate_probs, keep_mask, w_input, w_output):
    nx, nz = grid
    experts = nx * nz
    parts = lax.axis_size("mp")
    toks, model = activations.shape
    width = model // parts
    ff = w_input.shape[2]
    total = experts * CAP
    weights = (gate_probs * keep_mask.astype(jnp.float32)).T
    bf16 = jnp.bfloat16
    vmem = pl.BlockSpec(memory_space=pltpu.VMEM)
    hbm = pl.BlockSpec(memory_space=pl.ANY)
    dma = pltpu.SemaphoreType.DMA
    tokens, gwin, gwout = pl.pallas_call(
        functools.partial(kernel, nx, nz),
        name="moe_backward",
        out_shape=(
            jax.ShapeDtypeStruct((toks, width), bf16),
            jax.ShapeDtypeStruct((model, ff), bf16),
            jax.ShapeDtypeStruct((ff, model), bf16),
        ),
        in_specs=[vmem, vmem, hbm, hbm, hbm, hbm],
        out_specs=(vmem, hbm, hbm),
        scratch_shapes=[
            pltpu.VMEM((toks, width), bf16),
            pltpu.VMEM((toks, width), bf16),
            pltpu.VMEM((total, 2 * width), bf16),
            pltpu.VMEM((parts, total, 2 * width), bf16),
            pltpu.VMEM((model, ff), bf16),
            pltpu.VMEM((ff, model), bf16),
            pltpu.VMEM((parts, width, ff), bf16),
            pltpu.VMEM((parts, total, ff), bf16),
            pltpu.VMEM((total, ff), bf16),
            pltpu.VMEM((total, width), bf16),
            pltpu.VMEM((total, width), bf16),
            pltpu.VMEM((model, ff), bf16),
            pltpu.VMEM((ff, model), bf16),
            dma((4,)),
            dma(()),
            dma(()),
            dma((nx,)),
            dma((nx,)),
            dma((8, nx)),
            dma((nx,)),
            dma((nx,)),
            dma((2, nx)),
            dma((nx,)),
            dma((nx,)),
            dma((nx,)),
            dma(()),
            dma(()),
            dma((2,)),
        ],
        compiler_params=pltpu.CompilerParams(
            collective_id=0, has_side_effects=True, vmem_limit_bytes=48 * 2**20
        ),
        cost_estimate=pl.CostEstimate(
            flops=10 * total * model * ff, bytes_accessed=8 * model * ff * 2, transcendentals=total * ff
        ),
    )(expert_ids.T, weights, activations, out_grad, w_input[0], w_output[0])
    return (tokens, gwin[None], gwout[None])


def solution(mesh):
    grid = GRID[mesh.shape["expert"]]
    return jax.shard_map(
        functools.partial(local, grid),
        mesh=mesh,
        in_specs=(
            P("expert", None),
            P("expert", None),
            P("expert", None),
            P("expert", None),
            P("expert", None),
            P("expert", None, "mp"),
            P("expert", "mp", None),
        ),
        out_specs=(P("expert", "mp"), P("expert", None, "mp"), P("expert", "mp", None)),
        check_vma=False,
    )
```

```python
import functools
import math
import jax
import jax.numpy as jnp
from jax import lax
from jax.sharding import PartitionSpec as P
import jax.experimental.pallas as pl
import jax.experimental.pallas.tpu as pltpu

CAP = 16
NY = 4
MESH = pl.DeviceIdType.MESH
SCALE = math.sqrt(2.0 / math.pi)
CUBE = 0.044715

RINGED = 6
GROUPS = ((0, 1), (2, 3), (4,), (5,), (6, 7))
GRID = {
    32: (
        (4, 8),
        (
            ((0, 2), (1, 6), (2, 2), (3, 6)),
            ((0, 4), (1, 4), (2, 4), (3, 4)),
            ((0, 3), (1, 5), (2, 3), (3, 5)),
            ((0, 5), (1, 3), (2, 5), (3, 3)),
            ((0, 6), (1, 2), (2, 6), (3, 2)),
            ((1, 7), (2, 1), (2, 7), (3, 1)),
            ((0, 0), (1, 0), (2, 0), (3, 0)),
            ((0, 1), (0, 7), (1, 1), (3, 7)),
        ),
    ),
}


def contract_cols(left, right):
    return lax.dot_general(
        left, right, (((1,), (1,)), ((), ())), preferred_element_type=jnp.float32
    )


def product(left, right):
    return jnp.dot(left, right, preferred_element_type=jnp.float32)


def kernel(
    nx, nz, chunks,
    ids_hbm, gate_hbm, keep_hbm, act_hbm, grad_hbm, win_hbm, wout_hbm,
    tokens_out, gwin_v, gwout_v,
    ids_v, gate_v, keep_v, act_v, grad_v, sent, sent_near, rows, win_v, wout_v, win_all, hid_grad, active_v,
    back_sent, back,
    load_sem, win_send, win_recv, out_send, out_recv, ring_send, left_recv, right_recv,
    far_recv, core_recv, hid_send, hid_recv, pair_send, pair_recv, back_send, back_recv,
):
    experts = nx * nz
    toks, width = act_v.shape[1:]
    parts = 2 * NY
    total = rows.shape[2]
    span = total // len(chunks)
    count = len(chunks)
    final = GROUPS.index((RINGED - 1,))
    half = span // 2
    ff = win_v.shape[1]
    me_e = lax.axis_index("expert")
    me_m = lax.axis_index("mp")
    mx, mz = me_e // nz, lax.rem(me_e, nz)
    my, mc = me_m // 2, lax.rem(me_m, 2)

    def expert_at(dx, dz):
        return {"expert": lax.rem(mx + dx, nx) * nz + lax.rem(mz + dz, nz)}

    def up(dy):
        return lax.rem(my + dy, NY)

    right, left, far = up(1), up(NY - 1), up(2)
    other = {"mp": my * 2 + 1 - mc}

    def mate(y):
        return {"mp": y * 2 + mc}

    def column(y):
        return pl.ds(pl.multiple_of((y * 2 + mc) * width, width), width)

    small = [
        pltpu.make_async_copy(ids_hbm, ids_v, load_sem.at[2, 0]),
        pltpu.make_async_copy(gate_hbm, gate_v, load_sem.at[2, 1]),
        pltpu.make_async_copy(keep_hbm, keep_v, load_sem.at[2, 2]),
    ]
    for load in small:
        load.start()
    loads = []
    for dy in range(NY):
        y = up(dy)
        loads.append(pltpu.make_async_copy(act_hbm.at[:, column(y)], act_v.at[y], load_sem.at[0, dy]))
        loads.append(pltpu.make_async_copy(grad_hbm.at[:, column(y)], grad_v.at[y], load_sem.at[1, dy]))
    loads.append(pltpu.make_async_copy(win_hbm, win_v, load_sem.at[0, NY]))
    loads.append(pltpu.make_async_copy(wout_hbm, wout_v, load_sem.at[1, NY]))
    for load in loads:
        load.start()

    barrier = pltpu.get_barrier_semaphore()

    @pl.loop(1, experts)
    def _(step):
        pl.semaphore_signal(
            barrier, inc=1, device_id=expert_at(step // nz, lax.rem(step, nz)), device_id_type=MESH
        )

    @pl.loop(1, parts)
    def _(step):
        pl.semaphore_signal(
            barrier, inc=1, device_id={"mp": lax.rem(me_m + step, parts)}, device_id_type=MESH
        )

    for load in small:
        load.wait()
    ids = ids_v[...]
    weights = gate_v[...] * keep_v[...].astype(jnp.float32)
    lane_e = lax.broadcasted_iota(jnp.int32, (experts, toks), 0)
    chosen = [(lane_e == ids[k : k + 1, :]).astype(jnp.float32) for k in range(2)]
    before = lax.broadcasted_iota(jnp.int32, (toks, toks), 0)
    after = lax.broadcasted_iota(jnp.int32, (toks, toks), 1)
    upper = (before < after).astype(jnp.bfloat16)
    earlier = product((chosen[0] + chosen[1]).astype(jnp.bfloat16), upper)
    dx = lane_e // nz - mx
    dx = jnp.where(dx < 0, dx + nx, dx)
    dz = lane_e % nz - mz
    dz = jnp.where(dz < 0, dz + nz, dz)
    offset = dx * nz + dz
    base = jnp.zeros((experts, toks), jnp.float32)
    offsets = [pair for chunk in chunks for pair in chunk]
    for at, (ox, oz) in enumerate(offsets):
        base = jnp.where(offset == ox * nz + oz, float(at * CAP), base)
    places = [
        jnp.sum(chosen[k] * (earlier + base), axis=0, keepdims=True).astype(jnp.int32)
        for k in range(2)
    ]

    def select(start):
        lanes = lax.broadcasted_iota(jnp.int32, (span, toks), 0) + start
        hit = [lanes == places[k] for k in range(2)]
        picked = jnp.logical_or(hit[0], hit[1]).astype(jnp.float32)
        factor = jnp.where(hit[0], weights[0:1, :], 0.0) + jnp.where(hit[1], weights[1:2, :], 0.0)
        return picked, jnp.sum(factor, axis=1, keepdims=True)

    pl.semaphore_wait(barrier, experts - 1 + parts - 1)

    own = pl.ds(pl.multiple_of(me_m * width, width), width)
    pltpu.make_async_copy(win_hbm.at[own], win_all.at[me_m], win_recv).start()

    @pl.loop(1, parts)
    def _(step):
        to = lax.rem(me_m + step, parts)
        pltpu.make_async_remote_copy(
            win_hbm.at[pl.ds(pl.multiple_of(to * width, width), width)], win_all.at[me_m],
            win_send, win_recv, device_id={"mp": to}, device_id_type=MESH,
        ).start()

    def build(k):
        here = pl.ds(k * span, span)
        picked, factor = select(k * span)
        picked = picked.astype(jnp.bfloat16)
        sent[here, pl.ds(0, width)] = product(picked, act_v[my]).astype(jnp.bfloat16)
        sent[here, pl.ds(width, width)] = (factor * product(picked, grad_v[my])).astype(jnp.bfloat16)

    def launch(k):
        for at, (ox, oz) in enumerate(chunks[k]):
            here = pl.ds(k * span + at * CAP, CAP)
            pltpu.make_async_remote_copy(
                sent.at[here], rows.at[my, mc, here], out_send.at[k], out_recv.at[k],
                device_id=expert_at(ox, oz), device_id_type=MESH,
            ).start()

    def build_near(k):
        picked, factor = select(k * span)
        picked = picked.astype(jnp.bfloat16)
        for y in range(NY):
            wide = factor * product(picked, grad_v[y])
            sent_near[k - RINGED, y, :, pl.ds(0, width)] = product(picked, act_v[y]).astype(jnp.bfloat16)
            sent_near[k - RINGED, y, :, pl.ds(width, width)] = wide.astype(jnp.bfloat16)

    def launch_near(k):
        for at, (ox, oz) in enumerate(chunks[k]):
            here = pl.ds(k * span + at * CAP, CAP)
            source = sent_near.at[k - RINGED, :, pl.ds(at * CAP, CAP)]
            if (ox, oz) == (0, 0):
                pltpu.make_async_copy(source, rows.at[:, mc, here], out_recv.at[k]).start()
            else:
                pltpu.make_async_remote_copy(
                    source, rows.at[:, mc, here], out_send.at[k], out_recv.at[k],
                    device_id=expert_at(ox, oz), device_id_type=MESH,
                ).start()

    def launched(k):
        arrived(sent.at[pl.ds(k * span, span)], out_send.at[k])

    near_x, near_z = range(RINGED, count)
    loads[0].wait()
    loads[1].wait()
    build(0)
    launch(0)
    build(1)
    launch(1)
    for load in loads[2 : 2 * NY]:
        load.wait()
    build_near(near_x)
    launch_near(near_x)
    for k in range(2, RINGED):
        build(k)
    build_near(near_z)

    def launched_near(k):
        gone = span - CAP if (0, 0) in chunks[k] else span
        if gone:
            arrived(sent_near.at[k - RINGED, :, pl.ds(0, gone)], out_send.at[k])

    begun = []
    circling = []

    def push(ref, send, recv, device):
        copy = pltpu.make_async_remote_copy(
            ref, ref, send, recv, device_id=device, device_id_type=MESH
        )
        copy.start()
        begun.append(copy)
        return copy

    def arrived(ref, sem):
        pltpu.make_async_copy(ref, ref, sem).wait()

    def stage_own(k):
        ref = rows.at[my, mc, pl.ds(k * span, span)]
        arrived(ref, out_recv.at[k])
        if k > 1:
            for copy in circling[k - 2]:
                copy.wait_send()
        circling.append([
            push(ref, ring_send.at[0, k], left_recv.at[k], mate(right)),
            push(ref, ring_send.at[1, k], right_recv.at[k], mate(left)),
        ])
        if k < RINGED - 2:
            del begun[-2:]
        push(ref, ring_send.at[2, k], core_recv.at[k], other)

    def stage_side(k):
        at = k * span
        ref = rows.at[left, mc, pl.ds(at, span)]
        arrived(ref, left_recv.at[k])
        push(rows.at[left, mc, pl.ds(at, half)], ring_send.at[3, k], far_recv.at[0, k], mate(right))
        push(ref, ring_send.at[4, k], core_recv.at[k], other)
        ref = rows.at[right, mc, pl.ds(at, span)]
        arrived(ref, right_recv.at[k])
        push(rows.at[right, mc, pl.ds(at + half, half)], ring_send.at[5, k], far_recv.at[1, k], mate(left))
        push(ref, ring_send.at[6, k], core_recv.at[k], other)

    def stage_far(k):
        at = k * span
        arrived(rows.at[far, mc, pl.ds(at, half)], far_recv.at[0, k])
        arrived(rows.at[far, mc, pl.ds(at + half, half)], far_recv.at[1, k])
        push(rows.at[far, mc, pl.ds(at, span)], ring_send.at[7, k], core_recv.at[k], other)

    def stage_near(k):
        ref = rows.at[:, mc, pl.ds(k * span, span)]
        arrived(ref, out_recv.at[k])
        push(ref, ring_send.at[0, k], core_recv.at[k], other)

    def stage_hidden(k):
        at, size = GROUPS[k][0] * span, len(GROUPS[k]) * span
        for chunk in GROUPS[k]:
            arrived(rows.at[:, 0, pl.ds(chunk * span, span)], core_recv.at[chunk])

        def add(part, sums):
            hidden, grad_act = sums
            here = pl.ds(pl.multiple_of(part * width, width), width)
            block = rows[part // 2, lax.rem(part, 2), pl.ds(at, size), :]
            hidden = hidden + product(block[:, :width], win_v[here, :])
            grad_act = grad_act + contract_cols(block[:, width:], wout_v[:, here])
            return hidden, grad_act

        zero = jnp.zeros((size, ff), jnp.float32)
        hidden, grad_act = lax.fori_loop(0, parts, add, (zero, zero))
        square = hidden * hidden
        tanh = jnp.tanh(SCALE * (hidden + CUBE * (square * hidden)))
        active = 0.5 * hidden * (1.0 + tanh)
        slope = 0.5 * (1.0 + tanh) + 0.5 * hidden * (1.0 - tanh * tanh) * (
            SCALE * (1.0 + 3.0 * CUBE * square)
        )
        active_v[pl.ds(at, size), :] = active.astype(jnp.bfloat16)
        hid_grad[my, mc, pl.ds(at, size), :] = (grad_act * slope).astype(jnp.bfloat16)
        ref = hid_grad.at[my, mc, pl.ds(at, size)]
        if k == final:
            for step in range(1, parts):
                to = {"mp": lax.rem(me_m + step, parts)}
                push(ref, hid_send.at[step - 1, k], hid_recv.at[k], to)
        else:
            for side, y in enumerate((right, left, far)):
                push(ref, hid_send.at[side, k], hid_recv.at[k], mate(y))

    def stage_pair(k):
        at, size = GROUPS[k][0] * span, len(GROUPS[k]) * span
        arrived(hid_grad.at[pl.ds(0, NY - 1), 0, pl.ds(at, size)], hid_recv.at[k])
        push(hid_grad.at[:, mc, pl.ds(at, size)], pair_send.at[k], pair_recv.at[k], other)

    def stage_back(k):
        at, size = GROUPS[k][0] * span, len(GROUPS[k]) * span
        if k == final:
            arrived(hid_grad.at[0, 0, pl.ds(0, (parts - 1) * size)], hid_recv.at[k])
        else:
            arrived(hid_grad.at[:, 0, pl.ds(at, size)], pair_recv.at[k])
        grads = jnp.concatenate(
            [hid_grad[s // 2, s % 2, pl.ds(at, size), :] for s in range(parts)], axis=1
        )
        tile = min(256, width)

        @pl.loop(0, width // tile)
        def _(step):
            here = pl.ds(pl.multiple_of(step * tile, tile), tile)
            block = jnp.concatenate([win_all[s, here, :] for s in range(parts)], axis=1)
            back_sent[pl.ds(at, size), here] = contract_cols(grads, block).astype(jnp.bfloat16)

        for step, (ox, oz) in enumerate(offsets[at // CAP : (at + size) // CAP]):
            here = pl.ds(at + step * CAP, CAP)
            if (ox, oz) == (0, 0):
                pltpu.make_async_copy(back_sent.at[here], back.at[here], back_recv).start()
            else:
                pltpu.make_async_remote_copy(
                    back_sent.at[here], back.at[here], back_send, back_recv,
                    device_id=expert_at(nx - ox, nz - oz), device_id_type=MESH,
                ).start()

    tile = min(512, width)

    def grad_wout():
        active_t = active_v[...].astype(jnp.float32).T.astype(jnp.bfloat16)

        @pl.loop(0, parts)
        def _(part):
            for piece in range(0, width, tile):
                here = pl.ds(pl.multiple_of(part * width + piece, tile), tile)
                block = rows[part // 2, lax.rem(part, 2), :, pl.ds(width + piece, tile)]
                gwout_v[:, here] = product(active_t, block).astype(jnp.bfloat16)

    def grad_win():
        hid_t = hid_grad[my, mc].astype(jnp.float32).T.astype(jnp.bfloat16)

        @pl.loop(0, parts)
        def _(part):
            for piece in range(0, width, tile):
                here = pl.ds(pl.multiple_of(part * width + piece, tile), tile)
                block = rows[part // 2, lax.rem(part, 2), :, pl.ds(piece, tile)]
                gwin_v[here, :] = product(hid_t, block).T.astype(jnp.bfloat16)

    near = len(GROUPS) - 1
    launched(0)
    launch(2)
    stage_own(0)
    launched(1)
    launch(3)
    stage_own(1)
    stage_side(0)
    launched(2)
    launch(4)
    stage_near(near_x)
    stage_own(2)
    stage_side(1)
    stage_far(0)
    launched(3)
    launch(5)
    stage_own(3)
    launched(4)
    launch_near(near_z)
    stage_side(2)
    stage_far(1)
    for load in loads[2 * NY :]:
        load.wait()
    stage_hidden(0)
    stage_own(4)
    stage_side(3)
    stage_far(2)
    stage_pair(0)
    arrived(win_all, win_recv)
    stage_back(0)
    stage_own(5)
    stage_near(near_z)
    stage_side(4)
    stage_far(3)
    stage_hidden(near)
    stage_hidden(1)
    stage_side(5)
    stage_far(4)
    stage_pair(near)
    stage_pair(1)
    stage_hidden(2)
    stage_back(near)
    stage_back(1)
    stage_far(5)
    stage_pair(2)
    stage_hidden(3)
    stage_back(2)
    grad_wout()
    stage_back(3)
    grad_win()

    arrived(back, back_recv)
    sums = jnp.zeros((toks, width), jnp.float32)
    for k in range(count):
        picked, _ = select(k * span)
        sums = sums + product(picked.T.astype(jnp.bfloat16), back[pl.ds(k * span, span), :])
    tokens_out[...] = sums.astype(jnp.bfloat16)

    launched(5)
    launched_near(near_x)
    launched_near(near_z)
    arrived(win_all.at[pl.ds(0, parts - 1)], win_send)
    arrived(back_sent.at[pl.ds(0, total - CAP)], back_send)
    for copy in begun:
        copy.wait_send()


def local(grid, activations, out_grad, expert_ids, gate_probs, keep_mask, w_input, w_output):
    (nx, nz), chunks = grid
    count = len(chunks)
    parts = lax.axis_size("mp")
    toks, model = activations.shape
    width = model // parts
    ff = w_input.shape[2]
    total = nx * nz * CAP
    span = total // count
    bf16 = jnp.bfloat16
    vmem = pl.BlockSpec(memory_space=pltpu.VMEM)
    hbm = pl.BlockSpec(memory_space=pltpu.HBM)
    dma = pltpu.SemaphoreType.DMA
    tokens, gwin, gwout = pl.pallas_call(
        functools.partial(kernel, nx, nz, chunks),
        name="moe_backward",
        out_shape=(
            pltpu.VMEM((toks, width), bf16),
            pltpu.VMEM((model, ff), bf16),
            pltpu.VMEM((ff, model), bf16),
        ),
        in_specs=[hbm] * 7,
        out_specs=(vmem, vmem, vmem),
        scratch_shapes=[
            pltpu.VMEM((2, toks), jnp.int32),
            pltpu.VMEM((2, toks), jnp.float32),
            pltpu.VMEM((2, toks), jnp.int32),
            pltpu.VMEM((NY, toks, width), bf16),
            pltpu.VMEM((NY, toks, width), bf16),
            pltpu.VMEM((RINGED * span, 2 * width), bf16),
            pltpu.VMEM((count - RINGED, NY, span, 2 * width), bf16),
            pltpu.VMEM((NY, 2, total, 2 * width), bf16),
            pltpu.VMEM((model, ff), bf16),
            pltpu.VMEM((ff, model), bf16),
            pltpu.VMEM((parts, width, ff), bf16),
            pltpu.VMEM((NY, 2, total, ff), bf16),
            pltpu.VMEM((total, ff), bf16),
            pltpu.VMEM((total, width), bf16),
            pltpu.VMEM((total, width), bf16),
            dma((3, NY + 1)),
            dma(()),
            dma(()),
            dma((count,)),
            dma((count,)),
            dma((8, count)),
            dma((RINGED,)),
            dma((RINGED,)),
            dma((2, RINGED)),
            dma((count,)),
            dma((parts - 1, count)),
            dma((count,)),
            dma((count,)),
            dma((count,)),
            dma(()),
            dma(()),
        ],
        compiler_params=pltpu.CompilerParams(
            collective_id=0, has_side_effects=True, vmem_limit_bytes=50 * 2**20
        ),
        cost_estimate=pl.CostEstimate(
            flops=10 * total * model * ff, bytes_accessed=8 * model * ff * 2, transcendentals=total * ff
        ),
    )(expert_ids.T, gate_probs.T, keep_mask.T, activations, out_grad, w_input[0], w_output[0])
    return (tokens, gwin[None], gwout[None])


def solution(mesh):
    return jax.shard_map(
        functools.partial(local, GRID[mesh.shape["expert"]]),
        mesh=mesh,
        in_specs=(
            P("expert", None),
            P("expert", None),
            P("expert", None),
            P("expert", None),
            P("expert", None),
            P("expert", None, "mp"),
            P("expert", "mp", None),
        ),
        out_specs=(P("expert", "mp"), P("expert", None, "mp"), P("expert", "mp", None)),
        check_vma=False,
    )
```

```python
import functools
import math
import jax
import jax.numpy as jnp
from jax import lax
from jax.sharding import PartitionSpec as P
import jax.experimental.pallas as pl
import jax.experimental.pallas.tpu as pltpu

CAP = 16
NY = 4
MESH = pl.DeviceIdType.MESH
SCALE = math.sqrt(2.0 / math.pi)
CUBE = 0.044715

RINGED = 6
GROUPS = ((0, 1), (2, 3), (4,), (5,), (6, 7))
GRID = {
    32: (
        (4, 8),
        (
            ((0, 2), (1, 6), (2, 2), (3, 6)),
            ((0, 4), (1, 4), (2, 4), (3, 4)),
            ((0, 3), (1, 5), (2, 3), (3, 5)),
            ((0, 5), (1, 3), (2, 5), (3, 3)),
            ((0, 6), (1, 2), (2, 6), (3, 2)),
            ((0, 1), (0, 7), (1, 7), (3, 1)),
            ((0, 0), (1, 0), (2, 0), (3, 0)),
            ((1, 1), (2, 1), (2, 7), (3, 7)),
        ),
    ),
}


def contract_cols(left, right):
    return lax.dot_general(
        left, right, (((1,), (1,)), ((), ())), preferred_element_type=jnp.float32
    )


def product(left, right):
    return jnp.dot(left, right, preferred_element_type=jnp.float32)


def kernel(
    nx, nz, chunks,
    ids_hbm, gate_hbm, keep_hbm, act_hbm, grad_hbm, win_hbm, wout_hbm,
    tokens_out, gwin_v, gwout_v,
    ids_v, gate_v, keep_v, act_v, grad_v, sent, sent_near, rows, win_v, wout_v, win_all, hid_grad, active_v,
    back_sent, back,
    load_sem, win_send, win_recv, out_send, out_recv, ring_send, left_recv, right_recv,
    far_recv, core_recv, hid_send, hid_recv, pair_send, pair_recv, back_send, back_recv,
):
    experts = nx * nz
    toks, width = act_v.shape[1:]
    parts = 2 * NY
    total = rows.shape[2]
    sizes = [len(chunk) * CAP for chunk in chunks]
    starts = [sum(sizes[:k]) for k in range(len(chunks))]
    count = len(chunks)
    direct = (GROUPS.index((RINGED - 2,)), GROUPS.index((RINGED - 1,)))
    ff = win_v.shape[1]
    me_e = lax.axis_index("expert")
    me_m = lax.axis_index("mp")
    mx, mz = me_e // nz, lax.rem(me_e, nz)
    my, mc = me_m // 2, lax.rem(me_m, 2)

    def expert_at(dx, dz):
        return {"expert": lax.rem(mx + dx, nx) * nz + lax.rem(mz + dz, nz)}

    def up(dy):
        return lax.rem(my + dy, NY)

    right, left, far = up(1), up(NY - 1), up(2)
    other = {"mp": my * 2 + 1 - mc}

    def mate(y):
        return {"mp": y * 2 + mc}

    def column(y):
        return pl.ds(pl.multiple_of((y * 2 + mc) * width, width), width)

    barrier = pltpu.get_barrier_semaphore()

    @pl.loop(1, experts)
    def _(step):
        pl.semaphore_signal(
            barrier, inc=1, device_id=expert_at(step // nz, lax.rem(step, nz)), device_id_type=MESH
        )

    @pl.loop(1, parts)
    def _(step):
        pl.semaphore_signal(
            barrier, inc=1, device_id={"mp": lax.rem(me_m + step, parts)}, device_id_type=MESH
        )

    small = [
        pltpu.make_async_copy(ids_hbm, ids_v, load_sem.at[2, 0]),
        pltpu.make_async_copy(gate_hbm, gate_v, load_sem.at[2, 1]),
        pltpu.make_async_copy(keep_hbm, keep_v, load_sem.at[2, 2]),
    ]
    for load in small:
        load.start()
    loads = []
    for dy in range(NY):
        y = up(dy)
        loads.append(pltpu.make_async_copy(act_hbm.at[:, column(y)], act_v.at[y], load_sem.at[0, dy]))
        loads.append(pltpu.make_async_copy(grad_hbm.at[:, column(y)], grad_v.at[y], load_sem.at[1, dy]))
    loads.append(pltpu.make_async_copy(win_hbm, win_v, load_sem.at[0, NY]))
    loads.append(pltpu.make_async_copy(wout_hbm, wout_v, load_sem.at[1, NY]))
    for load in loads:
        load.start()

    pl.semaphore_wait(barrier, experts - 1 + parts - 1)

    own = pl.ds(pl.multiple_of(me_m * width, width), width)
    pltpu.make_async_copy(win_hbm.at[own], win_all.at[me_m], win_recv).start()

    @pl.loop(1, parts)
    def _(step):
        to = lax.rem(me_m + step, parts)
        pltpu.make_async_remote_copy(
            win_hbm.at[pl.ds(pl.multiple_of(to * width, width), width)], win_all.at[me_m],
            win_send, win_recv, device_id={"mp": to}, device_id_type=MESH,
        ).start()

    for load in small:
        load.wait()
    ids = ids_v[...]
    weights = gate_v[...] * keep_v[...].astype(jnp.float32)
    lane_e = lax.broadcasted_iota(jnp.int32, (experts, toks), 0)
    chosen = [(lane_e == ids[k : k + 1, :]).astype(jnp.float32) for k in range(2)]
    before = lax.broadcasted_iota(jnp.int32, (toks, toks), 0)
    after = lax.broadcasted_iota(jnp.int32, (toks, toks), 1)
    upper = (before < after).astype(jnp.bfloat16)
    earlier = product((chosen[0] + chosen[1]).astype(jnp.bfloat16), upper)
    dx = lane_e // nz - mx
    dx = jnp.where(dx < 0, dx + nx, dx)
    dz = lane_e % nz - mz
    dz = jnp.where(dz < 0, dz + nz, dz)
    offset = dx * nz + dz
    base = jnp.zeros((experts, toks), jnp.float32)
    offsets = [pair for chunk in chunks for pair in chunk]
    for at, (ox, oz) in enumerate(offsets):
        base = jnp.where(offset == ox * nz + oz, float(at * CAP), base)
    places = [
        jnp.sum(chosen[k] * (earlier + base), axis=0, keepdims=True).astype(jnp.int32)
        for k in range(2)
    ]

    def select(k):
        lanes = lax.broadcasted_iota(jnp.int32, (sizes[k], toks), 0) + starts[k]
        hit = [lanes == places[k] for k in range(2)]
        picked = jnp.logical_or(hit[0], hit[1]).astype(jnp.float32)
        factor = jnp.where(hit[0], weights[0:1, :], 0.0) + jnp.where(hit[1], weights[1:2, :], 0.0)
        return picked, jnp.sum(factor, axis=1, keepdims=True)

    def build(k):
        here = pl.ds(starts[k], sizes[k])
        picked, factor = select(k)
        picked = picked.astype(jnp.bfloat16)
        sent[here, pl.ds(0, width)] = product(picked, act_v[my]).astype(jnp.bfloat16)
        sent[here, pl.ds(width, width)] = (factor * product(picked, grad_v[my])).astype(jnp.bfloat16)

    def launch(k):
        for at, (ox, oz) in enumerate(chunks[k]):
            here = pl.ds(starts[k] + at * CAP, CAP)
            pltpu.make_async_remote_copy(
                sent.at[here], rows.at[my, mc, here], out_send.at[k], out_recv.at[k],
                device_id=expert_at(ox, oz), device_id_type=MESH,
            ).start()

    near_at = starts[RINGED]

    def build_near(k):
        picked, factor = select(k)
        picked = picked.astype(jnp.bfloat16)
        for y in range(NY):
            wide = factor * product(picked, grad_v[y])
            sent_near[y, pl.ds(starts[k] - near_at, sizes[k]), pl.ds(0, width)] = product(picked, act_v[y]).astype(jnp.bfloat16)
            sent_near[y, pl.ds(starts[k] - near_at, sizes[k]), pl.ds(width, width)] = wide.astype(jnp.bfloat16)

    def launch_near(k):
        for at, (ox, oz) in enumerate(chunks[k]):
            here = pl.ds(starts[k] + at * CAP, CAP)
            source = sent_near.at[:, pl.ds(starts[k] - near_at + at * CAP, CAP)]
            if (ox, oz) == (0, 0):
                pltpu.make_async_copy(source, rows.at[:, mc, here], out_recv.at[k]).start()
            else:
                pltpu.make_async_remote_copy(
                    source, rows.at[:, mc, here], out_send.at[k], out_recv.at[k],
                    device_id=expert_at(ox, oz), device_id_type=MESH,
                ).start()

    def launched(k):
        arrived(sent.at[pl.ds(starts[k], sizes[k])], out_send.at[k])

    near_x, near_z = range(RINGED, count)
    loads[0].wait()
    loads[1].wait()
    build(0)
    launch(0)
    build(1)
    launch(1)
    for load in loads[2 : 2 * NY]:
        load.wait()
    build_near(near_x)
    launch_near(near_x)
    for k in range(2, RINGED):
        build(k)
    build_near(near_z)

    def launched_near(k):
        gone = sizes[k] - CAP if (0, 0) in chunks[k] else sizes[k]
        if gone:
            arrived(sent_near.at[:, pl.ds(0, gone)], out_send.at[k])

    begun = []
    circling = []

    def push(ref, send, recv, device):
        copy = pltpu.make_async_remote_copy(
            ref, ref, send, recv, device_id=device, device_id_type=MESH
        )
        copy.start()
        begun.append(copy)
        return copy

    def arrived(ref, sem):
        pltpu.make_async_copy(ref, ref, sem).wait()

    def stage_own(k):
        ref = rows.at[my, mc, pl.ds(starts[k], sizes[k])]
        arrived(ref, out_recv.at[k])
        if k > 1:
            for copy in circling[k - 2]:
                copy.wait_send()
        circling.append([
            push(ref, ring_send.at[0, k], left_recv.at[k], mate(right)),
            push(ref, ring_send.at[1, k], right_recv.at[k], mate(left)),
        ])
        if k < RINGED - 2:
            del begun[-2:]
        push(ref, ring_send.at[2, k], core_recv.at[k], other)

    def stage_side(k):
        at, size, half = starts[k], sizes[k], sizes[k] // 2
        ref = rows.at[left, mc, pl.ds(at, size)]
        arrived(ref, left_recv.at[k])
        push(rows.at[left, mc, pl.ds(at, half)], ring_send.at[3, k], far_recv.at[0, k], mate(right))
        push(ref, ring_send.at[4, k], core_recv.at[k], other)
        ref = rows.at[right, mc, pl.ds(at, size)]
        arrived(ref, right_recv.at[k])
        push(rows.at[right, mc, pl.ds(at + half, half)], ring_send.at[5, k], far_recv.at[1, k], mate(left))
        push(ref, ring_send.at[6, k], core_recv.at[k], other)

    def stage_far(k):
        at, size, half = starts[k], sizes[k], sizes[k] // 2
        arrived(rows.at[far, mc, pl.ds(at, half)], far_recv.at[0, k])
        arrived(rows.at[far, mc, pl.ds(at + half, half)], far_recv.at[1, k])
        recv = core_recv.at[count if k == RINGED - 1 else k]
        push(rows.at[far, mc, pl.ds(at, size)], ring_send.at[7, k], recv, other)

    def stage_near(k):
        ref = rows.at[:, mc, pl.ds(starts[k], sizes[k])]
        arrived(ref, out_recv.at[k])
        push(ref, ring_send.at[0, k], core_recv.at[k], other)

    def place(k):
        return starts[GROUPS[k][0]], sum(sizes[chunk] for chunk in GROUPS[k])

    def add_part(y, core, here, sums):
        hidden, grad_act = sums
        part = pl.ds(pl.multiple_of((y * 2 + core) * width, width), width)
        block = rows[y, core, here, :]
        hidden = hidden + product(block[:, :width], win_v[part, :])
        grad_act = grad_act + contract_cols(block[:, width:], wout_v[:, part])
        return hidden, grad_act

    def stage_sums(k):
        at, size = place(k)
        here = pl.ds(at, size)
        zero = jnp.zeros((size, ff), jnp.float32)
        sums = (zero, zero)
        if GROUPS[k] == (RINGED - 1,):
            arrived(rows.at[pl.ds(0, NY - 1), 0, here], core_recv.at[RINGED - 1])
            for y in (my, left, right):
                sums = lax.fori_loop(0, 2, lambda core, held, y=y: add_part(y, core, here, held), sums)
            return sums
        for chunk in GROUPS[k]:
            arrived(rows.at[:, 0, pl.ds(starts[chunk], sizes[chunk])], core_recv.at[chunk])
        return lax.fori_loop(
            0, parts, lambda part, held: add_part(part // 2, lax.rem(part, 2), here, held), sums
        )

    def stage_hidden(k, sums=None):
        at, size = place(k)
        if sums is None:
            sums = stage_sums(k)
        else:
            here = pl.ds(at, size)
            arrived(rows.at[far, 1 - mc, here], core_recv.at[count])
            sums = lax.fori_loop(0, 2, lambda core, held: add_part(far, core, here, held), sums)
        hidden, grad_act = sums
        square = hidden * hidden
        tanh = jnp.tanh(SCALE * (hidden + CUBE * (square * hidden)))
        active = 0.5 * hidden * (1.0 + tanh)
        slope = 0.5 * (1.0 + tanh) + 0.5 * hidden * (1.0 - tanh * tanh) * (
            SCALE * (1.0 + 3.0 * CUBE * square)
        )
        active_v[pl.ds(at, size), :] = active.astype(jnp.bfloat16)
        hid_grad[my, mc, pl.ds(at, size), :] = (grad_act * slope).astype(jnp.bfloat16)
        ref = hid_grad.at[my, mc, pl.ds(at, size)]
        if k in direct:
            for step in range(1, parts):
                to = {"mp": lax.rem(me_m + step, parts)}
                push(ref, hid_send.at[step - 1, k], hid_recv.at[k], to)
        else:
            for side, y in enumerate((right, left, far)):
                push(ref, hid_send.at[side, k], hid_recv.at[k], mate(y))

    def stage_pair(k):
        at, size = place(k)
        arrived(hid_grad.at[pl.ds(0, NY - 1), 0, pl.ds(at, size)], hid_recv.at[k])
        push(hid_grad.at[:, mc, pl.ds(at, size)], pair_send.at[k], pair_recv.at[k], other)

    def stage_back(k):
        at, size = place(k)
        if k in direct:
            arrived(hid_grad.at[0, 0, pl.ds(0, (parts - 1) * size)], hid_recv.at[k])
        else:
            arrived(hid_grad.at[:, 0, pl.ds(at, size)], pair_recv.at[k])
        grads = jnp.concatenate(
            [hid_grad[s // 2, s % 2, pl.ds(at, size), :] for s in range(parts)], axis=1
        )
        tile = min(256, width)

        @pl.loop(0, width // tile)
        def _(step):
            here = pl.ds(pl.multiple_of(step * tile, tile), tile)
            block = jnp.concatenate([win_all[s, here, :] for s in range(parts)], axis=1)
            back_sent[pl.ds(at, size), here] = contract_cols(grads, block).astype(jnp.bfloat16)

        for step, (ox, oz) in enumerate(offsets[at // CAP : (at + size) // CAP]):
            here = pl.ds(at + step * CAP, CAP)
            if (ox, oz) == (0, 0):
                pltpu.make_async_copy(back_sent.at[here], back.at[here], back_recv.at[k]).start()
            else:
                pltpu.make_async_remote_copy(
                    back_sent.at[here], back.at[here], back_send, back_recv.at[k],
                    device_id=expert_at(nx - ox, nz - oz), device_id_type=MESH,
                ).start()

    tile = min(512, width)

    def grad_wout():
        active_t = active_v[...].astype(jnp.float32).T.astype(jnp.bfloat16)

        @pl.loop(0, parts)
        def _(part):
            for piece in range(0, width, tile):
                here = pl.ds(pl.multiple_of(part * width + piece, tile), tile)
                block = rows[part // 2, lax.rem(part, 2), :, pl.ds(width + piece, tile)]
                gwout_v[:, here] = product(active_t, block).astype(jnp.bfloat16)

    def grad_win():
        hid_t = hid_grad[my, mc].astype(jnp.float32).T.astype(jnp.bfloat16)

        @pl.loop(0, parts)
        def _(part):
            for piece in range(0, width, tile):
                here = pl.ds(pl.multiple_of(part * width + piece, tile), tile)
                block = rows[part // 2, lax.rem(part, 2), :, pl.ds(piece, tile)]
                gwin_v[here, :] = product(hid_t, block).T.astype(jnp.bfloat16)

    near = len(GROUPS) - 1
    launched(0)
    launch(2)
    stage_own(0)
    launched(1)
    launch(3)
    stage_own(1)
    stage_side(0)
    launched(2)
    launch(4)
    stage_near(near_x)
    stage_own(2)
    stage_side(1)
    stage_far(0)
    launched(3)
    launch(5)
    stage_own(3)
    launched(4)
    launch_near(near_z)
    stage_side(2)
    stage_far(1)
    for load in loads[2 * NY :]:
        load.wait()
    stage_hidden(0)
    stage_own(4)
    stage_side(3)
    stage_far(2)
    stage_pair(0)
    arrived(win_all, win_recv)
    stage_back(0)
    stage_own(5)
    stage_side(4)
    stage_far(3)
    stage_near(near_z)
    stage_hidden(1)
    stage_hidden(near)
    stage_side(5)
    stage_pair(1)
    stage_far(4)
    stage_pair(near)
    stage_back(1)
    stage_hidden(2)
    stage_back(near)
    part_sums = stage_sums(3)
    stage_far(5)
    stage_hidden(3, part_sums)
    stage_back(2)
    grad_wout()
    stage_back(3)
    grad_win()

    sums = jnp.zeros((toks, width), jnp.float32)
    for group in sorted(range(len(GROUPS)), key=lambda k: k in direct):
        at, size = place(group)
        arrived(back.at[pl.ds(at, size)], back_recv.at[group])
        for k in GROUPS[group]:
            picked, _ = select(k)
            mine = back[pl.ds(starts[k], sizes[k]), :]
            sums = sums + product(picked.T.astype(jnp.bfloat16), mine)
    tokens_out[...] = sums.astype(jnp.bfloat16)

    launched(5)
    launched_near(near_x)
    launched_near(near_z)
    arrived(win_all.at[pl.ds(0, parts - 1)], win_send)
    arrived(back_sent.at[pl.ds(0, total - CAP)], back_send)
    for copy in begun:
        copy.wait_send()


def local(grid, activations, out_grad, expert_ids, gate_probs, keep_mask, w_input, w_output):
    (nx, nz), chunks = grid
    count = len(chunks)
    parts = lax.axis_size("mp")
    toks, model = activations.shape
    width = model // parts
    ff = w_input.shape[2]
    total = nx * nz * CAP
    ringed = sum(len(chunk) for chunk in chunks[:RINGED]) * CAP
    bf16 = jnp.bfloat16
    vmem = pl.BlockSpec(memory_space=pltpu.VMEM)
    hbm = pl.BlockSpec(memory_space=pltpu.HBM)
    dma = pltpu.SemaphoreType.DMA
    tokens, gwin, gwout = pl.pallas_call(
        functools.partial(kernel, nx, nz, chunks),
        name="moe_backward",
        out_shape=(
            pltpu.VMEM((toks, width), bf16),
            pltpu.VMEM((model, ff), bf16),
            pltpu.VMEM((ff, model), bf16),
        ),
        in_specs=[hbm] * 7,
        out_specs=(vmem, vmem, vmem),
        scratch_shapes=[
            pltpu.VMEM((2, toks), jnp.int32),
            pltpu.VMEM((2, toks), jnp.float32),
            pltpu.VMEM((2, toks), jnp.int32),
            pltpu.VMEM((NY, toks, width), bf16),
            pltpu.VMEM((NY, toks, width), bf16),
            pltpu.VMEM((ringed, 2 * width), bf16),
            pltpu.VMEM((NY, total - ringed, 2 * width), bf16),
            pltpu.VMEM((NY, 2, total, 2 * width), bf16),
            pltpu.VMEM((model, ff), bf16),
            pltpu.VMEM((ff, model), bf16),
            pltpu.VMEM((parts, width, ff), bf16),
            pltpu.VMEM((NY, 2, total, ff), bf16),
            pltpu.VMEM((total, ff), bf16),
            pltpu.VMEM((total, width), bf16),
            pltpu.VMEM((total, width), bf16),
            dma((3, NY + 1)),
            dma(()),
            dma(()),
            dma((count,)),
            dma((count,)),
            dma((8, count)),
            dma((RINGED,)),
            dma((RINGED,)),
            dma((2, RINGED)),
            dma((count + 1,)),
            dma((parts - 1, count)),
            dma((count,)),
            dma((count,)),
            dma((count,)),
            dma(()),
            dma((count,)),
        ],
        compiler_params=pltpu.CompilerParams(
            collective_id=0, has_side_effects=True, vmem_limit_bytes=50 * 2**20
        ),
        cost_estimate=pl.CostEstimate(
            flops=10 * total * model * ff, bytes_accessed=8 * model * ff * 2, transcendentals=total * ff
        ),
    )(expert_ids.T, gate_probs.T, keep_mask.T, activations, out_grad, w_input[0], w_output[0])
    return (tokens, gwin[None], gwout[None])


def solution(mesh):
    return jax.shard_map(
        functools.partial(local, GRID[mesh.shape["expert"]]),
        mesh=mesh,
        in_specs=(
            P("expert", None),
            P("expert", None),
            P("expert", None),
            P("expert", None),
            P("expert", None),
            P("expert", None, "mp"),
            P("expert", "mp", None),
        ),
        out_specs=(P("expert", "mp"), P("expert", None, "mp"), P("expert", "mp", None)),
        check_vma=False,
    )
```

```python
import functools
import math
import jax
import jax.numpy as jnp
from jax import lax
from jax.sharding import PartitionSpec as P
import jax.experimental.pallas as pl
import jax.experimental.pallas.tpu as pltpu

CAP = 16
NY = 4
MESH = pl.DeviceIdType.MESH
SCALE = math.sqrt(2.0 / math.pi)
CUBE = 0.044715

RINGED = 6
GROUPS = ((0, 1), (2, 3), (4,), (5,), (6, 7))
GRID = {
    32: (
        (4, 8),
        (
            ((0, 2), (1, 6), (2, 2), (3, 6)),
            ((0, 4), (1, 4), (2, 4), (3, 4)),
            ((0, 3), (1, 5), (2, 3), (3, 5)),
            ((0, 5), (1, 3), (2, 5), (3, 3)),
            ((0, 6), (1, 2), (2, 6), (3, 2)),
            ((0, 1), (0, 7), (1, 7), (3, 1)),
            ((0, 0), (1, 0), (2, 0), (3, 0)),
            ((1, 1), (2, 1), (2, 7), (3, 7)),
        ),
    ),
}


def contract_cols(left, right):
    return lax.dot_general(
        left, right, (((1,), (1,)), ((), ())), preferred_element_type=jnp.float32
    )


def product(left, right):
    return jnp.dot(left, right, preferred_element_type=jnp.float32)


def kernel(
    nx, nz, chunks,
    ids_hbm, gate_hbm, keep_hbm, act_hbm, grad_hbm, win_hbm, wout_hbm,
    tokens_out, gwin_v, gwout_v,
    ids_v, gate_v, keep_v, act_v, grad_v, sent, sent_near, rows, win_v, wout_v, win_all, hid_grad, active_v,
    back_sent, back,
    load_sem, win_send, win_recv, out_send, out_recv, ring_send, left_recv, right_recv,
    far_recv, core_recv, hid_send, hid_recv, pair_send, pair_recv, back_send, back_recv,
):
    experts = nx * nz
    toks, width = act_v.shape[1:]
    parts = 2 * NY
    total = rows.shape[2]
    sizes = [len(chunk) * CAP for chunk in chunks]
    starts = [sum(sizes[:k]) for k in range(len(chunks))]
    count = len(chunks)
    direct = (GROUPS.index((RINGED - 2,)), GROUPS.index((RINGED - 1,)))
    ff = win_v.shape[1]
    me_e = lax.axis_index("expert")
    me_m = lax.axis_index("mp")
    mx, mz = me_e // nz, lax.rem(me_e, nz)
    my, mc = me_m // 2, lax.rem(me_m, 2)

    def expert_at(dx, dz):
        return {"expert": lax.rem(mx + dx, nx) * nz + lax.rem(mz + dz, nz)}

    def up(dy):
        return lax.rem(my + dy, NY)

    right, left, far = up(1), up(NY - 1), up(2)
    other = {"mp": my * 2 + 1 - mc}

    def mate(y):
        return {"mp": y * 2 + mc}

    def column(y):
        return pl.ds(pl.multiple_of((y * 2 + mc) * width, width), width)

    barrier = pltpu.get_barrier_semaphore()

    @pl.loop(1, experts)
    def _(step):
        pl.semaphore_signal(
            barrier, inc=1, device_id=expert_at(step // nz, lax.rem(step, nz)), device_id_type=MESH
        )

    @pl.loop(1, parts)
    def _(step):
        pl.semaphore_signal(
            barrier, inc=1, device_id={"mp": lax.rem(me_m + step, parts)}, device_id_type=MESH
        )

    small = [
        pltpu.make_async_copy(ids_hbm, ids_v, load_sem.at[2, 0]),
        pltpu.make_async_copy(gate_hbm, gate_v, load_sem.at[2, 1]),
        pltpu.make_async_copy(keep_hbm, keep_v, load_sem.at[2, 2]),
    ]
    for load in small:
        load.start()
    loads = []
    for dy in range(NY):
        y = up(dy)
        loads.append(pltpu.make_async_copy(act_hbm.at[:, column(y)], act_v.at[y], load_sem.at[0, dy]))
        loads.append(pltpu.make_async_copy(grad_hbm.at[:, column(y)], grad_v.at[y], load_sem.at[1, dy]))
    loads.append(pltpu.make_async_copy(win_hbm, win_v, load_sem.at[0, NY]))
    loads.append(pltpu.make_async_copy(wout_hbm, wout_v, load_sem.at[1, NY]))
    for load in loads:
        load.start()

    pl.semaphore_wait(barrier, experts - 1 + parts - 1)

    own = pl.ds(pl.multiple_of(me_m * width, width), width)
    pltpu.make_async_copy(win_hbm.at[own], win_all.at[me_m], win_recv).start()

    @pl.loop(1, parts)
    def _(step):
        to = lax.rem(me_m + step, parts)
        pltpu.make_async_remote_copy(
            win_hbm.at[pl.ds(pl.multiple_of(to * width, width), width)], win_all.at[me_m],
            win_send, win_recv, device_id={"mp": to}, device_id_type=MESH,
        ).start()

    for load in small:
        load.wait()
    ids = ids_v[...]
    weights = gate_v[...] * keep_v[...].astype(jnp.float32)
    lane_e = lax.broadcasted_iota(jnp.int32, (experts, toks), 0)
    chosen = [(lane_e == ids[k : k + 1, :]).astype(jnp.float32) for k in range(2)]
    before = lax.broadcasted_iota(jnp.int32, (toks, toks), 0)
    after = lax.broadcasted_iota(jnp.int32, (toks, toks), 1)
    upper = (before < after).astype(jnp.bfloat16)
    earlier = product((chosen[0] + chosen[1]).astype(jnp.bfloat16), upper)
    dx = lane_e // nz - mx
    dx = jnp.where(dx < 0, dx + nx, dx)
    dz = lane_e % nz - mz
    dz = jnp.where(dz < 0, dz + nz, dz)
    offset = dx * nz + dz
    base = jnp.zeros((experts, toks), jnp.float32)
    offsets = [pair for chunk in chunks for pair in chunk]
    for at, (ox, oz) in enumerate(offsets):
        base = jnp.where(offset == ox * nz + oz, float(at * CAP), base)
    places = [
        jnp.sum(chosen[k] * (earlier + base), axis=0, keepdims=True).astype(jnp.int32)
        for k in range(2)
    ]

    def select(k):
        lanes = lax.broadcasted_iota(jnp.int32, (sizes[k], toks), 0) + starts[k]
        hit = [lanes == places[k] for k in range(2)]
        picked = jnp.logical_or(hit[0], hit[1]).astype(jnp.float32)
        factor = jnp.where(hit[0], weights[0:1, :], 0.0) + jnp.where(hit[1], weights[1:2, :], 0.0)
        return picked, jnp.sum(factor, axis=1, keepdims=True)

    def build(k):
        here = pl.ds(starts[k], sizes[k])
        picked, factor = select(k)
        picked = picked.astype(jnp.bfloat16)
        sent[here, pl.ds(0, width)] = product(picked, act_v[my]).astype(jnp.bfloat16)
        sent[here, pl.ds(width, width)] = (factor * product(picked, grad_v[my])).astype(jnp.bfloat16)

    def launch(k):
        for at, (ox, oz) in enumerate(chunks[k]):
            here = pl.ds(starts[k] + at * CAP, CAP)
            pltpu.make_async_remote_copy(
                sent.at[here], rows.at[my, mc, here], out_send.at[k], out_recv.at[k],
                device_id=expert_at(ox, oz), device_id_type=MESH,
            ).start()

    near_at = starts[RINGED]

    def build_near(k):
        picked, factor = select(k)
        picked = picked.astype(jnp.bfloat16)
        for y in range(NY):
            wide = factor * product(picked, grad_v[y])
            sent_near[y, pl.ds(starts[k] - near_at, sizes[k]), pl.ds(0, width)] = product(picked, act_v[y]).astype(jnp.bfloat16)
            sent_near[y, pl.ds(starts[k] - near_at, sizes[k]), pl.ds(width, width)] = wide.astype(jnp.bfloat16)

    def launch_near(k):
        for at, (ox, oz) in enumerate(chunks[k]):
            here = pl.ds(starts[k] + at * CAP, CAP)
            source = sent_near.at[:, pl.ds(starts[k] - near_at + at * CAP, CAP)]
            if (ox, oz) == (0, 0):
                pltpu.make_async_copy(source, rows.at[:, mc, here], out_recv.at[k]).start()
            else:
                pltpu.make_async_remote_copy(
                    source, rows.at[:, mc, here], out_send.at[k], out_recv.at[k],
                    device_id=expert_at(ox, oz), device_id_type=MESH,
                ).start()

    def launched(k):
        arrived(sent.at[pl.ds(starts[k], sizes[k])], out_send.at[k])

    near_x, near_z = range(RINGED, count)
    loads[0].wait()
    loads[1].wait()
    build(0)
    launch(0)
    build(1)
    launch(1)
    for load in loads[2 : 2 * NY]:
        load.wait()
    build_near(near_x)
    launch_near(near_x)
    for k in range(2, RINGED):
        build(k)
    build_near(near_z)

    def launched_near(k):
        gone = sizes[k] - CAP if (0, 0) in chunks[k] else sizes[k]
        if gone:
            arrived(sent_near.at[:, pl.ds(0, gone)], out_send.at[k])

    begun = []
    circling = []

    def push(ref, send, recv, device):
        copy = pltpu.make_async_remote_copy(
            ref, ref, send, recv, device_id=device, device_id_type=MESH
        )
        copy.start()
        begun.append(copy)
        return copy

    def arrived(ref, sem):
        pltpu.make_async_copy(ref, ref, sem).wait()

    def stage_own(k):
        ref = rows.at[my, mc, pl.ds(starts[k], sizes[k])]
        arrived(ref, out_recv.at[k])
        if k > 1:
            for copy in circling[k - 2]:
                copy.wait_send()
        circling.append([
            push(ref, ring_send.at[0, k], left_recv.at[k], mate(right)),
            push(ref, ring_send.at[1, k], right_recv.at[k], mate(left)),
        ])
        if k < RINGED - 2:
            del begun[-2:]
        push(ref, ring_send.at[2, k], core_recv.at[k], other)

    def stage_side(k):
        at, size, half = starts[k], sizes[k], sizes[k] // 2
        ref = rows.at[left, mc, pl.ds(at, size)]
        arrived(ref, left_recv.at[k])
        push(rows.at[left, mc, pl.ds(at, half)], ring_send.at[3, k], far_recv.at[0, k], mate(right))
        push(ref, ring_send.at[4, k], core_recv.at[k], other)
        ref = rows.at[right, mc, pl.ds(at, size)]
        arrived(ref, right_recv.at[k])
        push(rows.at[right, mc, pl.ds(at + half, half)], ring_send.at[5, k], far_recv.at[1, k], mate(left))
        push(ref, ring_send.at[6, k], core_recv.at[k], other)

    def stage_far(k):
        at, size, half = starts[k], sizes[k], sizes[k] // 2
        arrived(rows.at[far, mc, pl.ds(at, half)], far_recv.at[0, k])
        arrived(rows.at[far, mc, pl.ds(at + half, half)], far_recv.at[1, k])
        recv = core_recv.at[count if k == RINGED - 1 else k]
        push(rows.at[far, mc, pl.ds(at, size)], ring_send.at[7, k], recv, other)

    def stage_near(k):
        ref = rows.at[:, mc, pl.ds(starts[k], sizes[k])]
        arrived(ref, out_recv.at[k])
        push(ref, ring_send.at[0, k], core_recv.at[k], other)

    def place(k):
        return starts[GROUPS[k][0]], sum(sizes[chunk] for chunk in GROUPS[k])

    def add_part(y, core, here, sums):
        hidden, grad_act = sums
        part = pl.ds(pl.multiple_of((y * 2 + core) * width, width), width)
        block = rows[y, core, here, :]
        hidden = hidden + product(block[:, :width], win_v[part, :])
        grad_act = grad_act + contract_cols(block[:, width:], wout_v[:, part])
        return hidden, grad_act

    def stage_sums(k):
        at, size = place(k)
        here = pl.ds(at, size)
        zero = jnp.zeros((size, ff), jnp.float32)
        sums = (zero, zero)
        if GROUPS[k] == (RINGED - 1,):
            arrived(rows.at[pl.ds(0, NY - 1), 0, here], core_recv.at[RINGED - 1])
            for y in (my, left, right):
                sums = lax.fori_loop(0, 2, lambda core, held, y=y: add_part(y, core, here, held), sums)
            return sums
        for chunk in GROUPS[k]:
            arrived(rows.at[:, 0, pl.ds(starts[chunk], sizes[chunk])], core_recv.at[chunk])
        return lax.fori_loop(
            0, parts, lambda part, held: add_part(part // 2, lax.rem(part, 2), here, held), sums
        )

    def stage_hidden(k, sums=None):
        at, size = place(k)
        if sums is None:
            sums = stage_sums(k)
        else:
            here = pl.ds(at, size)
            arrived(rows.at[far, 1 - mc, here], core_recv.at[count])
            sums = lax.fori_loop(0, 2, lambda core, held: add_part(far, core, here, held), sums)
        hidden, grad_act = sums
        square = hidden * hidden
        tanh = jnp.tanh(SCALE * (hidden + CUBE * (square * hidden)))
        active = 0.5 * hidden * (1.0 + tanh)
        slope = 0.5 * (1.0 + tanh) + 0.5 * hidden * (1.0 - tanh * tanh) * (
            SCALE * (1.0 + 3.0 * CUBE * square)
        )
        active_v[pl.ds(at, size), :] = active.astype(jnp.bfloat16)
        hid_grad[my, mc, pl.ds(at, size), :] = (grad_act * slope).astype(jnp.bfloat16)
        ref = hid_grad.at[my, mc, pl.ds(at, size)]
        if k in direct:
            for step in range(1, parts):
                to = {"mp": lax.rem(me_m + step, parts)}
                push(ref, hid_send.at[step - 1, k], hid_recv.at[k], to)
        else:
            for side, y in enumerate((right, left, far)):
                push(ref, hid_send.at[side, k], hid_recv.at[k], mate(y))

    def stage_pair(k):
        at, size = place(k)
        arrived(hid_grad.at[pl.ds(0, NY - 1), 0, pl.ds(at, size)], hid_recv.at[k])
        push(hid_grad.at[:, mc, pl.ds(at, size)], pair_send.at[k], pair_recv.at[k], other)

    def stage_back(k):
        at, size = place(k)
        if k in direct:
            arrived(hid_grad.at[0, 0, pl.ds(0, (parts - 1) * size)], hid_recv.at[k])
        else:
            arrived(hid_grad.at[:, 0, pl.ds(at, size)], pair_recv.at[k])
        grads = jnp.concatenate(
            [hid_grad[s // 2, s % 2, pl.ds(at, size), :] for s in range(parts)], axis=1
        )
        tile = min(256, width)

        @pl.loop(0, width // tile)
        def _(step):
            here = pl.ds(pl.multiple_of(step * tile, tile), tile)
            block = jnp.concatenate([win_all[s, here, :] for s in range(parts)], axis=1)
            back_sent[pl.ds(at, size), here] = contract_cols(grads, block).astype(jnp.bfloat16)

        for step, (ox, oz) in enumerate(offsets[at // CAP : (at + size) // CAP]):
            here = pl.ds(at + step * CAP, CAP)
            if (ox, oz) == (0, 0):
                pltpu.make_async_copy(back_sent.at[here], back.at[here], back_recv.at[k]).start()
            else:
                pltpu.make_async_remote_copy(
                    back_sent.at[here], back.at[here], back_send, back_recv.at[k],
                    device_id=expert_at(nx - ox, nz - oz), device_id_type=MESH,
                ).start()

    tile = min(512, width)

    def grad_wout():
        active_t = active_v[...].astype(jnp.float32).T.astype(jnp.bfloat16)

        @pl.loop(0, parts)
        def _(part):
            for piece in range(0, width, tile):
                here = pl.ds(pl.multiple_of(part * width + piece, tile), tile)
                block = rows[part // 2, lax.rem(part, 2), :, pl.ds(width + piece, tile)]
                gwout_v[:, here] = product(active_t, block).astype(jnp.bfloat16)

    def grad_win():
        hid_t = hid_grad[my, mc].astype(jnp.float32).T.astype(jnp.bfloat16)

        @pl.loop(0, parts)
        def _(part):
            for piece in range(0, width, tile):
                here = pl.ds(pl.multiple_of(part * width + piece, tile), tile)
                block = rows[part // 2, lax.rem(part, 2), :, pl.ds(piece, tile)]
                gwin_v[here, :] = product(hid_t, block).T.astype(jnp.bfloat16)

    near = len(GROUPS) - 1
    launched(0)
    launch(2)
    stage_own(0)
    launched(1)
    launch(3)
    stage_own(1)
    stage_side(0)
    launched(2)
    launch(4)
    stage_near(near_x)
    stage_own(2)
    stage_side(1)
    stage_far(0)
    launched(3)
    launch(5)
    stage_own(3)
    launched(4)
    launch_near(near_z)
    stage_side(2)
    stage_far(1)
    for load in loads[2 * NY :]:
        load.wait()
    stage_hidden(0)
    stage_own(4)
    stage_side(3)
    stage_own(5)
    stage_far(2)
    stage_pair(0)
    arrived(win_all, win_recv)
    stage_back(0)
    stage_side(4)
    stage_far(3)
    stage_near(near_z)
    stage_hidden(1)
    stage_hidden(near)
    stage_side(5)
    stage_pair(1)
    stage_far(4)
    stage_pair(near)
    stage_back(1)
    stage_hidden(2)
    stage_back(near)
    part_sums = stage_sums(3)
    stage_far(5)
    stage_hidden(3, part_sums)
    stage_back(2)
    grad_wout()
    stage_back(3)
    grad_win()

    sums = jnp.zeros((toks, width), jnp.float32)
    for group in sorted(range(len(GROUPS)), key=lambda k: k in direct):
        at, size = place(group)
        arrived(back.at[pl.ds(at, size)], back_recv.at[group])
        for k in GROUPS[group]:
            picked, _ = select(k)
            mine = back[pl.ds(starts[k], sizes[k]), :]
            sums = sums + product(picked.T.astype(jnp.bfloat16), mine)
    tokens_out[...] = sums.astype(jnp.bfloat16)

    launched(5)
    launched_near(near_x)
    launched_near(near_z)
    arrived(win_all.at[pl.ds(0, parts - 1)], win_send)
    arrived(back_sent.at[pl.ds(0, total - CAP)], back_send)
    for copy in begun:
        copy.wait_send()


def local(grid, activations, out_grad, expert_ids, gate_probs, keep_mask, w_input, w_output):
    (nx, nz), chunks = grid
    count = len(chunks)
    parts = lax.axis_size("mp")
    toks, model = activations.shape
    width = model // parts
    ff = w_input.shape[2]
    total = nx * nz * CAP
    ringed = sum(len(chunk) for chunk in chunks[:RINGED]) * CAP
    bf16 = jnp.bfloat16
    vmem = pl.BlockSpec(memory_space=pltpu.VMEM)
    hbm = pl.BlockSpec(memory_space=pltpu.HBM)
    dma = pltpu.SemaphoreType.DMA
    tokens, gwin, gwout = pl.pallas_call(
        functools.partial(kernel, nx, nz, chunks),
        name="moe_backward",
        out_shape=(
            pltpu.VMEM((toks, width), bf16),
            pltpu.VMEM((model, ff), bf16),
            pltpu.VMEM((ff, model), bf16),
        ),
        in_specs=[hbm] * 7,
        out_specs=(vmem, vmem, vmem),
        scratch_shapes=[
            pltpu.VMEM((2, toks), jnp.int32),
            pltpu.VMEM((2, toks), jnp.float32),
            pltpu.VMEM((2, toks), jnp.int32),
            pltpu.VMEM((NY, toks, width), bf16),
            pltpu.VMEM((NY, toks, width), bf16),
            pltpu.VMEM((ringed, 2 * width), bf16),
            pltpu.VMEM((NY, total - ringed, 2 * width), bf16),
            pltpu.VMEM((NY, 2, total, 2 * width), bf16),
            pltpu.VMEM((model, ff), bf16),
            pltpu.VMEM((ff, model), bf16),
            pltpu.VMEM((parts, width, ff), bf16),
            pltpu.VMEM((NY, 2, total, ff), bf16),
            pltpu.VMEM((total, ff), bf16),
            pltpu.VMEM((total, width), bf16),
            pltpu.VMEM((total, width), bf16),
            dma((3, NY + 1)),
            dma(()),
            dma(()),
            dma((count,)),
            dma((count,)),
            dma((8, count)),
            dma((RINGED,)),
            dma((RINGED,)),
            dma((2, RINGED)),
            dma((count + 1,)),
            dma((parts - 1, count)),
            dma((count,)),
            dma((count,)),
            dma((count,)),
            dma(()),
            dma((count,)),
        ],
        compiler_params=pltpu.CompilerParams(
            collective_id=0, has_side_effects=True, vmem_limit_bytes=50 * 2**20
        ),
        cost_estimate=pl.CostEstimate(
            flops=10 * total * model * ff, bytes_accessed=8 * model * ff * 2, transcendentals=total * ff
        ),
    )(expert_ids.T, gate_probs.T, keep_mask.T, activations, out_grad, w_input[0], w_output[0])
    return (tokens, gwin[None], gwout[None])


def solution(mesh):
    return jax.shard_map(
        functools.partial(local, GRID[mesh.shape["expert"]]),
        mesh=mesh,
        in_specs=(
            P("expert", None),
            P("expert", None),
            P("expert", None),
            P("expert", None),
            P("expert", None),
            P("expert", None, "mp"),
            P("expert", "mp", None),
        ),
        out_specs=(P("expert", "mp"), P("expert", None, "mp"), P("expert", "mp", None)),
        check_vma=False,
    )
```
